512 devices in a mesh: ctx: 128 (over z, x, y_lo), doc: 4 (over y_hi, core).
Axes of the slice: x: 4, y: 4 (y_hi: 2, y_lo: 2; y = y_hi * 2 + y_lo), z: 16, core: 2. Of those that a mesh axis runs over, the one named last changes fastest.
Arguments:
- teacher_hidden: bfloat16 [131072, 5120], P(('doc', 'ctx')), parts along dimension 0, may hold values from -6 to 6
- teacher_gain: float32 [5120], replicated, may hold values from 0.5 to 2
- group_proj: bfloat16 [5120, 512], P('ctx'), may hold values from -0.25 to 0.25
- student_hidden: bfloat16 [65536, 4096], P(('doc', 'ctx')), parts along dimension 0, may hold values from -6 to 6
- student_gain: float32 [4096], replicated, may hold values from 0.5 to 2
- student_count: int32 [512], P(('doc', 'ctx')), parts along dimension 0, may hold values from 64 to 128, as said below
- spans: int32 [65536, 8], P(('doc', 'ctx')), parts along dimension 0, may hold values from -1 to 32767, as said below
- span_len: int32 [65536], P(('doc', 'ctx')), parts along dimension 0, may hold values from 0 to 8, as said below
Outputs:
- grad_rows: bfloat16 [65536, 4096], P(('doc', 'ctx')), parts along dimension 0
- grad_gain: float32 [16384], P(('doc', 'ctx')), parts along dimension 0
- loss: float32 [4], P('doc'), parts along dimension 0
The draws below stay inside these ranges and needn't reach their ends.
There are 4 independent parts, one for each index of `doc`. The reference program is written for one: setup_inputs(seed, part) draws one part's arguments, and reference() takes and returns one part's arrays. A program takes and returns all parts, laid end to end along the dimension named above; an argument that names none is the same for every part. Nothing has to cross between parts.
Inputs may be any that keep to these rules, and one draw needn't show every extreme that they name: Slots 0 to student_count - 1 of a device's 128 slots hold tokens, the others are padding. `span_len`: 0 exactly on padding slots. `spans`: for a live slot on device i, entries 0 to span_len - 1 are consecutive rising teacher indices within i * 256 - 64 to (i + 1) * 256 + 63, clipped to the document; every other entry is -1.
All inputs are finite; a program needn't handle non-finite values.
Results may differ from the reference program's by a relative error of at most 0.0048.
Values may be sent and summed in bfloat16 or wider, within the bound.
No kernel may reach another device: no remote copies, remote signals or barrier semaphores. Data moves between devices by JAX's collectives and lax.ppermute only.
A program may use at most 64 MiB of HBM per device.

```python
import math
import jax
import jax.numpy as jnp
from jax import lax

HD = 128
TH = 40
SH = 32
KVG = 8
SPAN = 8
TT = 256
SC = 128
TG = 5
SG = 4
DT = 5120
DS = 4096
HALO = 64
TEACHER = 32768
SLOTS = 16384
N_CTX = 128


def live_counts(key):
    jitter_key = jax.random.fold_in(key, 11)
    spread = SC // 8
    lowest = max(SC // 2, 2)
    jitter = jax.random.randint(jitter_key, (N_CTX,), -spread, spread + 1)
    rising = lowest + (SC - lowest) * jnp.arange(N_CTX) // max(N_CTX - 1, 1)
    counts = jnp.clip(rising + jitter, lowest, SC)
    counts = counts.at[0].set(lowest)
    return counts.at[N_CTX - 1].set(SC).astype(jnp.int32)


def alignment(key):
    counts = live_counts(key)
    drifts = jax.random.randint(jax.random.fold_in(key, 21), (N_CTX,), -HALO, HALO - 6)
    drifts = drifts.at[1].set(-HALO).at[2].set(HALO - 7)
    lengths = jax.random.randint(jax.random.fold_in(key, 22), (N_CTX, SC), 1, SPAN + 1)
    lengths = lengths.at[2, counts[2] - 1].set(SPAN)
    position = jnp.arange(SC)
    live_slots = position[None, :] < counts[:, None]
    lengths = jnp.where(live_slots, lengths, 0)
    offsets = position[None, :] * (TT - 1) // jnp.maximum(counts - 1, 1)[:, None]
    starts = jnp.arange(N_CTX)[:, None] * TT + offsets + drifts[:, None]
    entry_index = jnp.arange(SPAN)
    index_table = jnp.clip(starts[:, :, None] + entry_index, 0, N_CTX * TT - 1)
    index_table = jnp.where(entry_index < lengths[:, :, None], index_table, -1)
    return (index_table.reshape(N_CTX * SC, SPAN).astype(jnp.int32), lengths.reshape(N_CTX * SC).astype(jnp.int32))


def draw_student_count(key, part):
    counts = live_counts(key)
    return counts


def draw_spans(key, part):
    index_table, lengths = alignment(key)
    return index_table


def draw_span_len(key, part):
    index_table, lengths = alignment(key)
    return lengths


def block_scale(stream_key, shape, split, low, largest):
    factor_of, own = 1.0, jax.random.fold_in(stream_key, 6)
    for dim, parts in split:
        draws = jnp.exp(jax.random.uniform(jax.random.fold_in(own, dim), (parts,), jnp.float32, low / len(split), largest / len(split)))
        factor_of = factor_of * jnp.repeat(draws, shape[dim] // parts).reshape([-1 if axis == dim else 1 for axis in range(len(shape))])
    return factor_of


def normal_values(stream_key, dims, scale, limit, shards=(), kind=jnp.bfloat16):
    result = scale * jax.random.normal(stream_key, dims, jnp.float32)
    if shards:
        result = result * block_scale(stream_key, dims, shards, -0.22, 0.18)
    return jnp.clip(result, -limit, limit).astype(kind)


def setup_inputs(seed: int = 0, part: int = 0) -> dict:
    splits = jax.random.split(jax.random.key(seed), 9)
    part_splits = jax.random.split(jax.random.fold_in(splits[8], part), 9)
    return {
        "teacher_hidden": normal_values(part_splits[0], (TEACHER, DT), 1.0, 6.0, ((0, 128),)),
        "teacher_gain": jnp.clip(jnp.exp(jax.random.uniform(splits[1], (DT,), jnp.float32, math.log(0.5), math.log(2.0))), 0.5, 2.0),
        "group_proj": normal_values(splits[2], (DT, SG * HD), (TG * HD) ** -0.5, 0.25, ((0, 128),)),
        "student_hidden": normal_values(part_splits[3], (SLOTS, DS), 1.0, 6.0, ((0, 128),)),
        "student_gain": jnp.clip(jnp.exp(jax.random.uniform(splits[4], (DS,), jnp.float32, math.log(0.5), math.log(2.0))), 0.5, 2.0),
        "student_count": draw_student_count(jax.random.fold_in(jax.random.fold_in(splits[8], part), 71), part),
        "spans": draw_spans(jax.random.fold_in(jax.random.fold_in(splits[8], part), 71), part),
        "span_len": draw_span_len(jax.random.fold_in(jax.random.fold_in(splits[8], part), 71), part),
    }


def project_block(teacher_block, teacher_gain, group_proj):
    teacher_float = teacher_block.astype(jnp.float32)
    teacher_scale = lax.rsqrt(lax.optimization_barrier(jnp.mean(teacher_float * teacher_float, axis=-1, keepdims=True)) + 1e-05)
    teacher_normed = (teacher_float * teacher_scale * teacher_gain).astype(jnp.bfloat16)
    split_rows = teacher_normed.astype(jnp.float32).reshape(teacher_block.shape[0], KVG, TG * HD)
    blocks = group_proj.astype(jnp.float32).reshape(KVG, TG * HD, SG * HD)
    mixed_rows = jnp.einsum('rgk,gkm->rgm', split_rows, blocks, precision=lax.Precision.HIGHEST)
    return mixed_rows.reshape(teacher_block.shape[0], SH * HD).astype(jnp.bfloat16)

def reference(teacher_hidden, teacher_gain, group_proj, student_hidden, student_gain, student_count, spans, span_len):
    blocks = teacher_hidden.reshape(N_CTX, TT, TH * HD)
    projected = lax.map(lambda teacher_block: project_block(teacher_block, teacher_gain, group_proj), blocks)
    projected = projected.reshape(TEACHER, SH * HD)
    pooled = jnp.zeros((spans.shape[0], SH * HD), jnp.float32)
    for column in range(SPAN):
        picked = jnp.clip(spans[:, column], 0, TEACHER - 1).astype(jnp.int32)
        weight_entry = (span_len > column).astype(jnp.float32)[:, None]
        pooled = pooled + projected[picked].astype(jnp.float32) * weight_entry
    pooled = pooled / jnp.maximum(span_len, 1).astype(jnp.float32)[:, None]
    slot_index = jnp.arange(spans.shape[0], dtype=jnp.int32)
    owner = (slot_index // SC).astype(jnp.int32)
    live_mask = (slot_index % SC < student_count[owner]).astype(jnp.float32)[:, None]
    student_float = student_hidden.astype(jnp.float32)
    inv_rms = lax.rsqrt(lax.optimization_barrier(jnp.mean(student_float * student_float, axis=-1, keepdims=True)) + 1e-05)
    normed_student = student_float * inv_rms
    mismatch = live_mask * (normed_student * student_gain - pooled)
    live_total = jnp.sum(student_count.astype(jnp.float32))
    loss = (jnp.sum(mismatch * mismatch) / (SH * HD * live_total)).reshape(1)
    grad_gain = lax.optimization_barrier(jnp.sum(mismatch * normed_student, axis=0)) / live_total
    scaled = mismatch * student_gain
    inner_mean = lax.optimization_barrier(jnp.mean(scaled * normed_student, axis=-1, keepdims=True))
    grad_rows = (inv_rms * (scaled - normed_student * inner_mean)).astype(jnp.bfloat16)
    return (grad_rows, grad_gain, loss)
```

```python
import jax
import jax.numpy as jnp
from jax import lax
from jax.sharding import Mesh
from jax.sharding import PartitionSpec as P

HD = 128
SH = 32
KVG = 8
SPAN = 8
TG = 5
SG = 4
HALO = 64
NZ = 16
NX = 4
NY = 2
CTX = ("z", "x", "ylo")
PART = ("yhi", "core")
SWAP = [(0, 1), (1, 0)]


def shared(cells, count):
    return jnp.broadcast_to(cells[None], (count,) + cells.shape)


def gather_columns(group_proj):
    half = SG * HD // 2
    mine = lax.dynamic_slice_in_dim(group_proj, lax.axis_index("core") * half, half, axis=1)
    line = lax.all_to_all(shared(mine, NZ), "z", 0, 0)
    plane = lax.all_to_all(shared(line, NX * NY), ("x", "ylo"), 0, 0)
    return plane.transpose(1, 0, 2, 3).reshape(KVG, TG * HD, half)


def normalize(teacher_hidden, teacher_gain):
    teacher_float = teacher_hidden.astype(jnp.float32)
    teacher_scale = lax.rsqrt(
        jnp.mean(teacher_float * teacher_float, axis=-1, keepdims=True) + 1e-05
    )
    return (teacher_float * teacher_scale * teacher_gain).astype(jnp.bfloat16)


def per_device(
    teacher_hidden,
    teacher_gain,
    group_proj,
    student_hidden,
    student_gain,
    student_count,
    spans,
    span_len,
):
    row_count = teacher_hidden.shape[0]
    slot_count = student_hidden.shape[0]
    half = SG * HD // 2
    core = lax.axis_index("core")
    devices = NZ * NX * NY

    up = [(i, (i + 1) % devices) for i in range(devices)]
    down = [((i + 1) % devices, i) for i in range(devices)]
    lower = lax.ppermute(teacher_hidden[row_count - HALO :], CTX, up)
    upper = lax.ppermute(teacher_hidden[:HALO], CTX, down)

    weights = gather_columns(group_proj)

    offset_rows = lax.axis_index(CTX) * row_count - HALO
    local_index = spans - offset_rows
    live_entry = jnp.arange(SPAN, dtype=jnp.int32)[None, :] < span_len[:, None]
    local_index = jnp.where(live_entry, local_index, -1)

    def counts(first, rows):
        wanted = jnp.arange(rows, dtype=jnp.int32) + first
        hits = local_index[:, :, None] == wanted[None, None, :]
        return jnp.sum(hits.astype(jnp.float32), axis=1).astype(jnp.bfloat16)

    def summed(first, rows):
        return jnp.dot(
            counts(first, rows.shape[0]),
            normalize(rows, teacher_gain),
            preferred_element_type=jnp.float32,
        )

    total = summed(HALO, teacher_hidden)
    total = total + summed(0, lower)
    total = total + summed(HALO + row_count, upper)
    share = 1.0 / jnp.maximum(span_len, 1).astype(jnp.float32)[:, None]
    pooled_normed = (total * share).astype(jnp.bfloat16)

    other_normed = lax.ppermute(pooled_normed, "core", SWAP)
    both = jnp.concatenate([pooled_normed, other_normed], axis=0)
    both = both.reshape(2 * slot_count, KVG, TG * HD)
    mixed = jnp.einsum("rgk,gkm->rgm", both, weights, preferred_element_type=jnp.float32)
    own = mixed[:slot_count].astype(jnp.bfloat16)
    back = lax.ppermute(mixed[slot_count:].astype(jnp.bfloat16), "core", SWAP)
    low = jnp.where(core == 0, own, back)
    high = jnp.where(core == 0, back, own)
    pooled = jnp.concatenate([low, high], axis=2).reshape(slot_count, SH * HD)
    pooled = pooled.astype(jnp.float32)

    live_mask = (jnp.arange(slot_count, dtype=jnp.int32) < student_count[0]).astype(jnp.float32)[
        :, None
    ]
    student_float = student_hidden.astype(jnp.float32)
    inv_rms = lax.rsqrt(jnp.mean(student_float * student_float, axis=-1, keepdims=True) + 1e-05)
    normed_student = student_float * inv_rms
    mismatch = live_mask * (normed_student * student_gain - pooled)
    scaled = mismatch * student_gain
    inner_mean = jnp.mean(scaled * normed_student, axis=-1, keepdims=True)
    grad_rows = (inv_rms * (scaled - normed_student * inner_mean)).astype(jnp.bfloat16)
    gain_terms = jnp.sum(mismatch * normed_student, axis=0)
    square_local = jnp.sum(mismatch * mismatch)
    count_local = student_count.astype(jnp.float32)[0]

    piece = SH * HD // devices
    terms = gain_terms.reshape(NZ, NX * NY, piece).transpose(1, 0, 2)
    tail = jnp.broadcast_to(
        jnp.stack([square_local, count_local])[None, None, :], (NX * NY, NZ, 2)
    )
    terms = jnp.concatenate([terms, tail], axis=2)
    terms = jnp.sum(lax.all_to_all(terms, ("x", "ylo"), 0, 0), axis=0)
    terms = jnp.sum(lax.all_to_all(terms, "z", 0, 0), axis=0)
    live_total = terms[piece + 1]
    grad_gain = terms[:piece] / live_total
    loss = (terms[piece] / (SH * HD * live_total)).reshape(1)
    return (grad_rows, grad_gain, loss)


def solution(mesh):
    fine = Mesh(mesh.devices.reshape(NZ, NX, NY, 2, 2), CTX + PART)
    every = PART + CTX
    placed = (
        P(every, None),
        P(),
        P(CTX, None),
        P(every, None),
        P(),
        P(every),
        P(every, None),
        P(every),
    )
    return jax.shard_map(
        per_device,
        mesh=fine,
        in_specs=placed,
        out_specs=(P(every, None), P(every), P(PART)),
        check_vma=False,
    )
```

```python
import jax
import jax.numpy as jnp
from jax import lax
from jax.experimental import pallas as pl
from jax.experimental.pallas import tpu as pltpu
from jax.sharding import Mesh
from jax.sharding import PartitionSpec as P

HD = 128
SH = 32
KVG = 8
SPAN = 8
TG = 5
SG = 4
HALO = 64
NZ = 16
NX = 4
NY = 2
CTX = ("z", "x", "ylo")
PART = ("yhi", "core")
DEVICES = NZ * NX * NY
SWAP = [(0, 1), (1, 0)]
WIDE = SG * HD
HALF = WIDE // 2
LANES = 128
PIECE = SH * HD // DEVICES


def shared(cells, count):
    return jnp.broadcast_to(cells[None], (count,) + cells.shape)


def gather_columns(group_proj):
    mine = lax.dynamic_slice_in_dim(group_proj, lax.axis_index("core") * HALF, HALF, axis=1)
    line = lax.all_to_all(shared(mine, NZ), "z", 0, 0)
    groups = [[x * 4 + lo * 2 + (lo ^ k) for x in range(NX) for lo in range(NY)] for k in range(2)]
    plane = lax.all_to_all(
        shared(line, NX * NY), ("x", "ylo", "yhi"), 0, 0, axis_index_groups=groups
    )
    return plane.transpose(1, 0, 2, 3).reshape(KVG, TG * HD, HALF), line


def normalize(teacher_hidden, teacher_gain):
    teacher_float = teacher_hidden.astype(jnp.float32)
    teacher_scale = lax.rsqrt(
        jnp.mean(teacher_float * teacher_float, axis=-1, keepdims=True) + 1e-05
    )
    return (teacher_float * teacher_scale * teacher_gain).astype(jnp.bfloat16)


def mismatch_block(group, core_ref, count_ref, student_ref, inv, gain_ref, own_ref, back_ref):
    slots = student_ref.shape[0]
    wide = slice(group * WIDE, (group + 1) * WIDE)
    own = own_ref[group].astype(jnp.float32)
    back = back_ref[group].astype(jnp.float32)
    first = core_ref[0] == 0
    low = jnp.where(first, own, back)
    high = jnp.where(first, back, own)
    pooled = jnp.concatenate([low, high], axis=1)
    normed = student_ref[:, wide].astype(jnp.float32) * inv
    live = lax.broadcasted_iota(jnp.int32, (slots, 1), 0) < count_ref[0]
    gain = gain_ref[:, wide]
    mismatch = jnp.where(live, normed * gain - pooled, 0.0)
    return normed, mismatch, gain


def sums_kernel(
    core_ref, count_ref, student_ref, inv_ref, gain_ref, own_ref, back_ref, terms_ref, inner_ref
):
    slots = student_ref.shape[0]
    inv = inv_ref[...]
    inner = jnp.zeros((slots, LANES), jnp.float32)
    square = jnp.zeros((1, LANES), jnp.float32)
    per = LANES // PIECE
    blocks = []
    for group in range(KVG):
        normed, mismatch, gain = mismatch_block(
            group, core_ref, count_ref, student_ref, inv, gain_ref, own_ref, back_ref
        )
        product = mismatch * normed
        weighted = product * gain
        sums = jnp.sum(product, axis=0, keepdims=True)
        squares = jnp.sum(mismatch * mismatch, axis=0, keepdims=True)
        for tile in range(WIDE // LANES):
            part = slice(tile * LANES, (tile + 1) * LANES)
            inner = inner + weighted[:, part]
            square = square + squares[:, part]
            lanes = sums[:, part]
            for turn in range(per):
                blocks.append(lanes if turn == 0 else pltpu.roll(lanes, LANES - turn * PIECE, 1))
    inner_ref[...] = jnp.sum(inner, axis=1, keepdims=True)
    block = jnp.concatenate(blocks, axis=0)
    lane = lax.broadcasted_iota(jnp.int32, block.shape, 1)
    total = jnp.sum(square, axis=1, keepdims=True)
    live = count_ref[0].astype(jnp.float32)
    block = jnp.where(lane < PIECE, block, 0.0)
    block = jnp.where(lane == PIECE, total, block)
    terms_ref[...] = jnp.where(lane == PIECE + 1, live, block)


def rows_kernel(
    core_ref, count_ref, student_ref, inv_ref, gain_ref, own_ref, back_ref, inner_ref, grad_ref
):
    inv = inv_ref[...]
    mean = inner_ref[...] * (1.0 / (SH * HD))
    for group in range(KVG):
        normed, mismatch, gain = mismatch_block(
            group, core_ref, count_ref, student_ref, inv, gain_ref, own_ref, back_ref
        )
        grad = inv * (mismatch * gain - normed * mean)
        grad_ref[:, group * WIDE : (group + 1) * WIDE] = grad.astype(grad_ref.dtype)


def per_device(
    teacher_hidden,
    teacher_gain,
    group_proj,
    student_hidden,
    student_gain,
    student_count,
    spans,
    span_len,
):
    row_count = teacher_hidden.shape[0]
    slot_count = student_hidden.shape[0]
    core = lax.axis_index("core")
    lo = lax.axis_index("ylo")

    within = [(i, i ^ 1) for i in range(DEVICES)]
    across = [(i, (i + 1 if i % 2 else i - 1) % DEVICES) for i in range(DEVICES)]
    head = teacher_hidden[:HALO]
    tail = teacher_hidden[row_count - HALO :]
    inner = lax.ppermute(jnp.where(lo == 0, tail, head), CTX, within)
    outer = lax.ppermute(jnp.where(lo == 0, head, tail), CTX, across)

    weights, line = gather_columns(group_proj)
    teacher_hidden = lax.optimization_barrier((teacher_hidden, line))[0]
    inner = lax.optimization_barrier((inner, line))[0]
    outer = lax.optimization_barrier((outer, line))[0]

    offset_rows = lax.axis_index(CTX) * row_count - HALO
    local_index = spans - offset_rows
    live_entry = jnp.arange(SPAN, dtype=jnp.int32)[None, :] < span_len[:, None]
    local_index = jnp.where(live_entry, local_index, -1)

    def counts(first, rows):
        wanted = jnp.arange(rows, dtype=jnp.int32) + first
        hits = local_index[:, :, None] == wanted[None, None, :]
        return jnp.sum(hits.astype(jnp.float32), axis=1).astype(jnp.bfloat16)

    def summed(first, rows):
        return jnp.dot(
            counts(first, rows.shape[0]),
            normalize(rows, teacher_gain),
            preferred_element_type=jnp.float32,
        )

    total = summed(HALO, teacher_hidden)
    total = total + summed(jnp.where(lo == 0, HALO + row_count, 0), inner)
    total = total + summed(jnp.where(lo == 0, 0, HALO + row_count), outer)
    share = 1.0 / jnp.maximum(span_len, 1).astype(jnp.float32)[:, None]
    pooled_normed = (total * share).astype(jnp.bfloat16)

    other_normed = lax.ppermute(pooled_normed, "core", SWAP)
    pooled_normed = pooled_normed.reshape(slot_count, KVG, TG * HD)
    other_normed = other_normed.reshape(slot_count, KVG, TG * HD)

    def projected(rows):
        mixed = jnp.einsum("rgk,gkm->grm", rows, weights, preferred_element_type=jnp.float32)
        return mixed.astype(jnp.bfloat16)

    back = lax.ppermute(projected(other_normed), "core", SWAP)
    own = projected(pooled_normed)

    student_float = student_hidden.astype(jnp.float32)
    inv_rms = lax.rsqrt(jnp.mean(student_float * student_float, axis=-1, keepdims=True) + 1e-05)
    operands = (
        core.astype(jnp.int32).reshape(1),
        student_count,
        student_hidden,
        inv_rms,
        student_gain.reshape(1, SH * HD),
        own,
        back,
    )
    scalar = pl.BlockSpec(memory_space=pltpu.SMEM)
    whole = pl.BlockSpec(memory_space=pltpu.VMEM)
    limit = pltpu.CompilerParams(vmem_limit_bytes=32 * 1024 * 1024)
    terms, inner_sum = pl.pallas_call(
        sums_kernel,
        in_specs=[scalar, scalar] + [whole] * 5,
        out_specs=[whole, whole],
        out_shape=[
            jax.ShapeDtypeStruct((DEVICES, LANES), jnp.float32),
            jax.ShapeDtypeStruct((slot_count, 1), jnp.float32),
        ],
        compiler_params=limit,
        cost_estimate=pl.CostEstimate(flops=8_000_000, bytes_accessed=2_200_000, transcendentals=0),
    )(*operands)
    grad_rows = pl.pallas_call(
        rows_kernel,
        in_specs=[scalar, scalar] + [whole] * 6,
        out_specs=whole,
        out_shape=jax.ShapeDtypeStruct((slot_count, SH * HD), jnp.bfloat16),
        compiler_params=limit,
        cost_estimate=pl.CostEstimate(flops=8_000_000, bytes_accessed=3_200_000, transcendentals=0),
    )(*operands, inner_sum)

    terms = jnp.sum(lax.all_to_all(terms, CTX, 0, 0, tiled=True), axis=0)
    live_total = terms[PIECE + 1]
    grad_gain = terms[:PIECE] / live_total
    loss = (terms[PIECE] / (SH * HD * live_total)).reshape(1)
    return (grad_rows, grad_gain, loss)


def solution(mesh):
    fine = Mesh(mesh.devices.reshape(NZ, NX, NY, 2, 2), CTX + PART)
    every = PART + CTX
    placed = (
        P(every, None),
        P(),
        P(CTX, None),
        P(every, None),
        P(),
        P(every),
        P(every, None),
        P(every),
    )
    return jax.shard_map(
        per_device,
        mesh=fine,
        in_specs=placed,
        out_specs=(P(every, None), P(every), P(PART)),
        check_vma=False,
    )
```

```python
import jax
import jax.numpy as jnp
from jax import lax
from jax.experimental import pallas as pl
from jax.experimental.pallas import tpu as pltpu
from jax.sharding import Mesh
from jax.sharding import PartitionSpec as P

HD = 128
SH = 32
KVG = 8
SPAN = 8
TG = 5
SG = 4
HALO = 64
NZ = 16
NX = 4
NY = 2
CTX = ("z", "x", "ylo")
PART = ("yhi", "core")
DEVICES = NZ * NX * NY
SWAP = [(0, 1), (1, 0)]
WIDE = SG * HD
HALF = WIDE // 2
LANES = 128
PIECE = SH * HD // DEVICES


def shared(cells, count):
    return jnp.broadcast_to(cells[None], (count,) + cells.shape)


def gather_columns(group_proj):
    mine = lax.dynamic_slice_in_dim(group_proj, lax.axis_index("core") * HALF, HALF, axis=1)
    line = lax.all_to_all(shared(mine, NZ), "z", 0, 0)
    groups = [[x * 4 + lo * 2 + (lo ^ k) for x in range(NX) for lo in range(NY)] for k in range(2)]
    plane = lax.all_to_all(
        shared(line, NX * NY), ("x", "ylo", "yhi"), 0, 0, axis_index_groups=groups
    )
    return plane.transpose(1, 0, 2, 3).reshape(KVG, TG * HD, HALF), line


def normalize(teacher_hidden, teacher_gain):
    teacher_float = teacher_hidden.astype(jnp.float32)
    teacher_scale = lax.rsqrt(
        jnp.mean(teacher_float * teacher_float, axis=-1, keepdims=True) + 1e-05
    )
    return (teacher_float * teacher_scale * teacher_gain).astype(jnp.bfloat16)


def mismatch_block(group, core_ref, count_ref, student_ref, inv, gain_ref, own_ref, back_ref):
    slots = student_ref.shape[0]
    wide = slice(group * WIDE, (group + 1) * WIDE)
    own = own_ref[group].astype(jnp.float32)
    back = back_ref[group].astype(jnp.float32)
    first = core_ref[0] == 0
    low = jnp.where(first, own, back)
    high = jnp.where(first, back, own)
    pooled = jnp.concatenate([low, high], axis=1)
    normed = student_ref[:, wide].astype(jnp.float32) * inv
    live = lax.broadcasted_iota(jnp.int32, (slots, 1), 0) < count_ref[0]
    gain = gain_ref[:, wide]
    mismatch = jnp.where(live, normed * gain - pooled, 0.0)
    return normed, mismatch, gain


def sums_kernel(
    core_ref, count_ref, student_ref, inv_ref, gain_ref, own_ref, back_ref, terms_ref, inner_ref
):
    slots = student_ref.shape[0]
    inv = inv_ref[...]
    inner = jnp.zeros((slots, LANES), jnp.float32)
    square = jnp.zeros((1, LANES), jnp.float32)
    per = LANES // PIECE
    blocks = []
    for group in range(KVG):
        normed, mismatch, gain = mismatch_block(
            group, core_ref, count_ref, student_ref, inv, gain_ref, own_ref, back_ref
        )
        product = mismatch * normed
        weighted = product * gain
        sums = jnp.sum(product, axis=0, keepdims=True)
        squares = jnp.sum(mismatch * mismatch, axis=0, keepdims=True)
        for tile in range(WIDE // LANES):
            part = slice(tile * LANES, (tile + 1) * LANES)
            inner = inner + weighted[:, part]
            square = square + squares[:, part]
            lanes = sums[:, part]
            for turn in range(per):
                blocks.append(lanes if turn == 0 else pltpu.roll(lanes, LANES - turn * PIECE, 1))
    inner_ref[...] = jnp.sum(inner, axis=1, keepdims=True)
    block = jnp.concatenate(blocks, axis=0)
    lane = lax.broadcasted_iota(jnp.int32, block.shape, 1)
    total = jnp.sum(square, axis=1, keepdims=True)
    live = count_ref[0].astype(jnp.float32)
    block = jnp.where(lane < PIECE, block, 0.0)
    block = jnp.where(lane == PIECE, total, block)
    terms_ref[...] = jnp.where(lane == PIECE + 1, live, block)


def rows_kernel(
    core_ref, count_ref, student_ref, inv_ref, gain_ref, own_ref, back_ref, inner_ref, grad_ref
):
    inv = inv_ref[...]
    mean = inner_ref[...] * (1.0 / (SH * HD))
    for group in range(KVG):
        normed, mismatch, gain = mismatch_block(
            group, core_ref, count_ref, student_ref, inv, gain_ref, own_ref, back_ref
        )
        grad = inv * (mismatch * gain - normed * mean)
        grad_ref[:, group * WIDE : (group + 1) * WIDE] = grad.astype(grad_ref.dtype)


def total_kernel(terms_ref, grad_ref, loss_ref):
    total = jnp.sum(terms_ref[...], axis=0)
    live = jnp.sum(terms_ref[:, PIECE + 1 : PIECE + 2])
    grad_ref[...] = total[:PIECE] / live
    loss_ref[...] = total[PIECE : PIECE + 1] / (SH * HD * live)


def per_device(
    teacher_hidden,
    teacher_gain,
    group_proj,
    student_hidden,
    student_gain,
    student_count,
    spans,
    span_len,
):
    row_count = teacher_hidden.shape[0]
    slot_count = student_hidden.shape[0]
    core = lax.axis_index("core")
    lo = lax.axis_index("ylo")

    within = [(i, i ^ 1) for i in range(DEVICES)]
    across = [(i, i + 1 if i % 2 else i - 1) for i in range(1, DEVICES - 1)]
    head = teacher_hidden[:HALO]
    tail = teacher_hidden[row_count - HALO :]
    inner = lax.ppermute(jnp.where(lo == 0, tail, head), CTX, within)
    outer = lax.ppermute(jnp.where(lo == 0, head, tail), CTX, across)

    weights, line = gather_columns(group_proj)
    teacher_hidden = lax.optimization_barrier((teacher_hidden, line))[0]
    inner = lax.optimization_barrier((inner, line))[0]
    outer = lax.optimization_barrier((outer, line))[0]

    offset_rows = lax.axis_index(CTX) * row_count - HALO
    local_index = spans - offset_rows
    live_entry = jnp.arange(SPAN, dtype=jnp.int32)[None, :] < span_len[:, None]
    local_index = jnp.where(live_entry, local_index, -1)

    def counts(first, rows):
        wanted = jnp.arange(rows, dtype=jnp.int32) + first
        hits = local_index[:, :, None] == wanted[None, None, :]
        return jnp.sum(hits.astype(jnp.float32), axis=1).astype(jnp.bfloat16)

    def summed(first, rows):
        return jnp.dot(
            counts(first, rows.shape[0]),
            normalize(rows, teacher_gain),
            preferred_element_type=jnp.float32,
        )

    total = summed(HALO, teacher_hidden)
    total = total + summed(jnp.where(lo == 0, HALO + row_count, 0), inner)
    total = total + summed(jnp.where(lo == 0, 0, HALO + row_count), outer)
    share = 1.0 / jnp.maximum(span_len, 1).astype(jnp.float32)[:, None]
    pooled_normed = (total * share).astype(jnp.bfloat16)

    other_normed = lax.ppermute(pooled_normed, "core", SWAP)
    pooled_normed = pooled_normed.reshape(slot_count, KVG, TG * HD)
    other_normed = other_normed.reshape(slot_count, KVG, TG * HD)

    def projected(rows):
        mixed = jnp.einsum("rgk,gkm->grm", rows, weights, preferred_element_type=jnp.float32)
        return mixed.astype(jnp.bfloat16)

    back = lax.ppermute(projected(other_normed), "core", SWAP)
    own = projected(pooled_normed)

    student_float = student_hidden.astype(jnp.float32)
    inv_rms = lax.rsqrt(jnp.mean(student_float * student_float, axis=-1, keepdims=True) + 1e-05)
    operands = (
        core.astype(jnp.int32).reshape(1),
        student_count,
        student_hidden,
        inv_rms,
        student_gain.reshape(1, SH * HD),
        own,
        back,
    )
    scalar = pl.BlockSpec(memory_space=pltpu.SMEM)
    whole = pl.BlockSpec(memory_space=pltpu.VMEM)
    limit = pltpu.CompilerParams(vmem_limit_bytes=32 * 1024 * 1024)
    terms, inner_sum = pl.pallas_call(
        sums_kernel,
        in_specs=[scalar, scalar] + [whole] * 5,
        out_specs=[whole, whole],
        out_shape=[
            jax.ShapeDtypeStruct((DEVICES, LANES), jnp.float32),
            jax.ShapeDtypeStruct((slot_count, 1), jnp.float32),
        ],
        compiler_params=limit,
        cost_estimate=pl.CostEstimate(flops=8_000_000, bytes_accessed=2_200_000, transcendentals=0),
    )(*operands)
    grad_rows = pl.pallas_call(
        rows_kernel,
        in_specs=[scalar, scalar] + [whole] * 6,
        out_specs=whole,
        out_shape=jax.ShapeDtypeStruct((slot_count, SH * HD), jnp.bfloat16),
        compiler_params=limit,
        cost_estimate=pl.CostEstimate(flops=8_000_000, bytes_accessed=3_200_000, transcendentals=0),
    )(*operands, inner_sum)

    terms = lax.all_to_all(terms, CTX, 0, 0, tiled=True)
    grad_gain, loss = pl.pallas_call(
        total_kernel,
        in_specs=[whole],
        out_specs=[whole, whole],
        out_shape=[
            jax.ShapeDtypeStruct((PIECE,), jnp.float32),
            jax.ShapeDtypeStruct((1,), jnp.float32),
        ],
    )(terms)
    return (grad_rows, grad_gain, loss)


def solution(mesh):
    fine = Mesh(mesh.devices.reshape(NZ, NX, NY, 2, 2), CTX + PART)
    every = PART + CTX
    placed = (
        P(every, None),
        P(),
        P(CTX, None),
        P(every, None),
        P(),
        P(every),
        P(every, None),
        P(every),
    )
    return jax.shard_map(
        per_device,
        mesh=fine,
        in_specs=placed,
        out_specs=(P(every, None), P(every), P(PART)),
        check_vma=False,
    )
```

```python
import jax
import jax.numpy as jnp
from jax import lax
from jax.experimental import pallas as pl
from jax.experimental.pallas import tpu as pltpu
from jax.sharding import Mesh
from jax.sharding import PartitionSpec as P

HD = 128
SH = 32
KVG = 8
SPAN = 8
TG = 5
SG = 4
HALO = 64
NZ = 16
NX = 4
NY = 2
CTX = ("z", "x", "ylo")
PART = ("yhi", "core")
DEVICES = NZ * NX * NY
SWAP = [(0, 1), (1, 0)]
WIDE = SG * HD
HALF = WIDE // 2
LANES = 128
PIECE = SH * HD // DEVICES


def shared(cells, count):
    return jnp.broadcast_to(cells[None], (count,) + cells.shape)


def gather_columns(group_proj):
    mine = lax.dynamic_slice_in_dim(group_proj, lax.axis_index("core") * HALF, HALF, axis=1)
    line = lax.all_to_all(shared(mine, NZ), "z", 0, 0)
    groups = [[x * 4 + lo * 2 + (lo ^ k) for x in range(NX) for lo in range(NY)] for k in range(2)]
    plane = lax.all_to_all(
        shared(line, NX * NY), ("x", "ylo", "yhi"), 0, 0, axis_index_groups=groups
    )
    return plane.transpose(1, 0, 2, 3).reshape(KVG, TG * HD, HALF), line


def normalize(teacher_hidden, teacher_gain):
    teacher_float = teacher_hidden.astype(jnp.float32)
    teacher_scale = lax.rsqrt(
        jnp.mean(teacher_float * teacher_float, axis=-1, keepdims=True) + 1e-05
    )
    return (teacher_float * teacher_scale * teacher_gain).astype(jnp.bfloat16)


def mismatch_block(group, core_ref, count_ref, student_ref, inv, gain_ref, own_ref, back_ref):
    slots = student_ref.shape[0]
    wide = slice(group * WIDE, (group + 1) * WIDE)
    own = own_ref[group].astype(jnp.float32)
    back = back_ref[group].astype(jnp.float32)
    first = core_ref[0] == 0
    low = jnp.where(first, own, back)
    high = jnp.where(first, back, own)
    pooled = jnp.concatenate([low, high], axis=1)
    normed = student_ref[:, wide].astype(jnp.float32) * inv
    live = lax.broadcasted_iota(jnp.int32, (slots, 1), 0) < count_ref[0]
    gain = gain_ref[:, wide]
    mismatch = jnp.where(live, normed * gain - pooled, 0.0)
    return normed, mismatch, gain


def sums_kernel(
    core_ref, count_ref, student_ref, inv_ref, gain_ref, own_ref, back_ref, terms_ref, inner_ref
):
    slots = student_ref.shape[0]
    inv = inv_ref[...]
    inner = jnp.zeros((slots, LANES), jnp.float32)
    square = jnp.zeros((1, LANES), jnp.float32)
    per = LANES // PIECE
    blocks = []
    for group in range(KVG):
        normed, mismatch, gain = mismatch_block(
            group, core_ref, count_ref, student_ref, inv, gain_ref, own_ref, back_ref
        )
        product = mismatch * normed
        weighted = product * gain
        sums = jnp.sum(product, axis=0, keepdims=True)
        squares = jnp.sum(mismatch * mismatch, axis=0, keepdims=True)
        for tile in range(WIDE // LANES):
            part = slice(tile * LANES, (tile + 1) * LANES)
            inner = inner + weighted[:, part]
            square = square + squares[:, part]
            lanes = sums[:, part]
            for turn in range(per):
                blocks.append(lanes if turn == 0 else pltpu.roll(lanes, LANES - turn * PIECE, 1))
    inner_ref[...] = jnp.sum(inner, axis=1, keepdims=True)
    block = jnp.concatenate(blocks, axis=0)
    lane = lax.broadcasted_iota(jnp.int32, block.shape, 1)
    total = jnp.sum(square, axis=1, keepdims=True)
    live = count_ref[0].astype(jnp.float32)
    block = jnp.where(lane < PIECE, block, 0.0)
    block = jnp.where(lane == PIECE, total, block)
    terms_ref[...] = jnp.where(lane == PIECE + 1, live, block)


def rows_kernel(
    core_ref, count_ref, student_ref, inv_ref, gain_ref, own_ref, back_ref, inner_ref, grad_ref
):
    inv = inv_ref[...]
    mean = inner_ref[...] * (1.0 / (SH * HD))
    for group in range(KVG):
        normed, mismatch, gain = mismatch_block(
            group, core_ref, count_ref, student_ref, inv, gain_ref, own_ref, back_ref
        )
        grad = inv * (mismatch * gain - normed * mean)
        grad_ref[:, group * WIDE : (group + 1) * WIDE] = grad.astype(grad_ref.dtype)


def total_kernel(terms_ref, grad_ref, loss_ref):
    total = jnp.sum(terms_ref[...], axis=0)
    live = jnp.sum(terms_ref[:, PIECE + 1 : PIECE + 2])
    grad_ref[...] = total[:PIECE] / live
    loss_ref[...] = total[PIECE : PIECE + 1] / (SH * HD * live)


def per_device(
    teacher_hidden,
    teacher_gain,
    group_proj,
    student_hidden,
    student_gain,
    student_count,
    spans,
    span_len,
):
    row_count = teacher_hidden.shape[0]
    slot_count = student_hidden.shape[0]
    core = lax.axis_index("core")
    lo = lax.axis_index("ylo")

    within = [(i, i ^ 1) for i in range(DEVICES)]
    across = [(i, i + 1 if i % 2 else i - 1) for i in range(1, DEVICES - 1)]
    head = teacher_hidden[:HALO]
    tail = teacher_hidden[row_count - HALO :]
    far = jnp.where(lo == 0, head, tail)
    outer = lax.ppermute(far, CTX, across)
    near = lax.optimization_barrier((jnp.where(lo == 0, tail, head), far))[0]
    inner = lax.ppermute(near, CTX, within)

    weights, line = gather_columns(group_proj)
    teacher_hidden = lax.optimization_barrier((teacher_hidden, line))[0]
    inner = lax.optimization_barrier((inner, line))[0]
    outer = lax.optimization_barrier((outer, line))[0]

    offset_rows = lax.axis_index(CTX) * row_count - HALO
    local_index = spans - offset_rows
    live_entry = jnp.arange(SPAN, dtype=jnp.int32)[None, :] < span_len[:, None]
    local_index = jnp.where(live_entry, local_index, -1)

    def counts(first, rows):
        wanted = jnp.arange(rows, dtype=jnp.int32) + first
        hits = local_index[:, :, None] == wanted[None, None, :]
        return jnp.sum(hits.astype(jnp.float32), axis=1).astype(jnp.bfloat16)

    def summed(first, rows):
        return jnp.dot(
            counts(first, rows.shape[0]),
            normalize(rows, teacher_gain),
            preferred_element_type=jnp.float32,
        )

    total = summed(HALO, teacher_hidden)
    total = total + summed(jnp.where(lo == 0, HALO + row_count, 0), inner)
    total = total + summed(jnp.where(lo == 0, 0, HALO + row_count), outer)
    share = 1.0 / jnp.maximum(span_len, 1).astype(jnp.float32)[:, None]
    pooled_normed = (total * share).astype(jnp.bfloat16)

    other_normed = lax.ppermute(pooled_normed, "core", SWAP)
    pooled_normed = pooled_normed.reshape(slot_count, KVG, TG * HD)
    other_normed = other_normed.reshape(slot_count, KVG, TG * HD)

    def projected(rows):
        mixed = jnp.einsum("rgk,gkm->grm", rows, weights, preferred_element_type=jnp.float32)
        return mixed.astype(jnp.bfloat16)

    back = lax.ppermute(projected(other_normed), "core", SWAP)
    own = projected(pooled_normed)

    student_float = student_hidden.astype(jnp.float32)
    inv_rms = lax.rsqrt(jnp.mean(student_float * student_float, axis=-1, keepdims=True) + 1e-05)
    operands = (
        core.astype(jnp.int32).reshape(1),
        student_count,
        student_hidden,
        inv_rms,
        student_gain.reshape(1, SH * HD),
        own,
        back,
    )
    scalar = pl.BlockSpec(memory_space=pltpu.SMEM)
    whole = pl.BlockSpec(memory_space=pltpu.VMEM)
    limit = pltpu.CompilerParams(vmem_limit_bytes=32 * 1024 * 1024)
    terms, inner_sum = pl.pallas_call(
        sums_kernel,
        in_specs=[scalar, scalar] + [whole] * 5,
        out_specs=[whole, whole],
        out_shape=[
            jax.ShapeDtypeStruct((DEVICES, LANES), jnp.float32),
            jax.ShapeDtypeStruct((slot_count, 1), jnp.float32),
        ],
        compiler_params=limit,
        cost_estimate=pl.CostEstimate(flops=8_000_000, bytes_accessed=2_200_000, transcendentals=0),
    )(*operands)
    grad_rows = pl.pallas_call(
        rows_kernel,
        in_specs=[scalar, scalar] + [whole] * 6,
        out_specs=whole,
        out_shape=jax.ShapeDtypeStruct((slot_count, SH * HD), jnp.bfloat16),
        compiler_params=limit,
        cost_estimate=pl.CostEstimate(flops=8_000_000, bytes_accessed=3_200_000, transcendentals=0),
    )(*operands, inner_sum)

    terms = lax.all_to_all(terms, CTX, 0, 0, tiled=True)
    grad_gain, loss = pl.pallas_call(
        total_kernel,
        in_specs=[whole],
        out_specs=[whole, whole],
        out_shape=[
            jax.ShapeDtypeStruct((PIECE,), jnp.float32),
            jax.ShapeDtypeStruct((1,), jnp.float32),
        ],
    )(terms)
    return (grad_rows, grad_gain, loss)


def solution(mesh):
    fine = Mesh(mesh.devices.reshape(NZ, NX, NY, 2, 2), CTX + PART)
    every = PART + CTX
    placed = (
        P(every, None),
        P(),
        P(CTX, None),
        P(every, None),
        P(),
        P(every),
        P(every, None),
        P(every),
    )
    return jax.shard_map(
        per_device,
        mesh=fine,
        in_specs=placed,
        out_specs=(P(every, None), P(every), P(PART)),
        check_vma=False,
    )
```
